32 devices in a mesh: grp: 4 (over y, x), ing: 8 (over z, core).
Axes of the slice: x: 2, y: 2, z: 4, core: 2. Of those that a mesh axis runs over, the one named last changes fastest.
Arguments:
- tokens: bfloat16 [4096, 14848], P(('grp', 'ing')), may hold values from -6 to 6
- ln_gain: float32 [14848], replicated, may hold values from 0.1 to 1.9
- ln_bias: float32 [14848], replicated, may hold values from -3 to 3
- master: float32 [14848, 512], P(('ing', 'grp')), may hold values from -0.046875 to 0.046875
- grad: bfloat16 [14848, 512], P(('ing', 'grp')), may hold values from -6 to 6
- moment1: float32 [14848, 512], P(('ing', 'grp')), may hold values from -0.6 to 0.6
- moment2: float32 [14848, 512], P(('ing', 'grp')), may hold values from 0.02 to 0.2
Outputs:
- new_master: float32 [14848, 512], P(('ing', 'grp'))
- new_moment1: float32 [14848, 512], P(('ing', 'grp'))
- new_moment2: float32 [14848, 512], P(('ing', 'grp'))
- keys: bfloat16 [4096, 512], P(('grp', 'ing'))
The draws below stay inside these ranges and needn't reach their ends.
All inputs are finite; a program needn't handle non-finite values.
Results may differ from the reference program's by a relative error of at most 0.012.
Values may be sent and summed in bfloat16 or wider, within the bound.
A program may use at most 128 MiB of HBM per device.

```python
import math
import jax
import jax.numpy as jnp
from jax import lax

D = 14848
QBLOCK = 128
KEYS = 512
TOKENS = 4096


def steps_of(rng, dims, shards, least, largest):
    def one(dim, blocks):
        steps = jax.random.uniform(jax.random.fold_in(jax.random.fold_in(rng, 6), dim), (blocks,), jnp.float32, least / len(shards), largest / len(shards))
        return jnp.repeat(jnp.exp(steps), dims[dim] // blocks).reshape((-1,) + (1,) * (len(dims) - dim - 1))

    factor_of = one(*shards[0])
    for cut in shards[1:]:
        factor_of = factor_of * one(*cut)
    return factor_of


def centred(own_key, shape, scale, bound, shards=(), dtype=jnp.bfloat16):
    array = scale * jax.random.normal(own_key, shape, jnp.float32)
    if shards:
        array = array * steps_of(own_key, shape, shards, -0.22, 0.18)
    return jnp.clip(array, -bound, bound).astype(dtype)


def setup_inputs(seed: int = 0) -> dict:
    seeds = jax.random.split(jax.random.key(seed), 8)
    return {
        "tokens": centred(seeds[0], (TOKENS, D), 1.0, 6.0, ((0, 32),)),
        "ln_gain": jnp.clip(1.0 + 0.18 * jax.random.normal(seeds[1], (D,), jnp.float32), 0.1, 1.9),
        "ln_bias": centred(seeds[2], (D,), 0.5, 3.0, (), jnp.float32),
        "master": centred(seeds[3], (D, KEYS), D ** -0.5, 0.046875, ((0, 32),), jnp.float32),
        "grad": centred(seeds[4], (D, KEYS), 1.0, 6.0, ((0, 32),)),
        "moment1": centred(seeds[5], (D, KEYS), 0.1, 0.6, ((0, 32),), jnp.float32),
        "moment2": jnp.clip(jnp.exp(math.log(0.2) - 2.3025851 * jax.random.uniform(seeds[6], (D, KEYS), jnp.float32) ** steps_of(seeds[6], (D, KEYS), ((0, 32),), -0.2, 0.2)), 0.02, 0.2),
    }


def adam_update(master, grad, moment1, moment2):
    gradient = grad.astype(jnp.float32)
    first = 0.9 * moment1 + 0.1 * gradient
    second = 0.95 * moment2 + 0.05 * gradient * gradient
    step_size = first / 0.19 / (jnp.sqrt(second / 0.0975) + 1e-08)
    updated = master - 0.008 * (step_size + 0.1 * master)
    return (updated, first, second)

def block_scale(updated):
    rows, width = updated.shape
    blocked = updated.reshape(rows, width // QBLOCK, QBLOCK)
    scale = ((lax.optimization_barrier(jnp.max(jnp.abs(blocked), axis=2)) + 1e-06) / 127.0).astype(jnp.bfloat16)
    quant = (blocked / scale.astype(jnp.float32)[:, :, None]).astype(jnp.bfloat16)
    weight = quant.astype(jnp.float32) * scale.astype(jnp.float32)[:, :, None]
    return weight.reshape(rows, width).astype(jnp.bfloat16)

def reference(tokens, ln_gain, ln_bias, master, grad, moment1, moment2):
    new_master, new_moment1, new_moment2 = adam_update(master, grad, moment1, moment2)
    weight = block_scale(new_master)
    block_rows = min(TOKENS, 4096)
    blocks = tokens.reshape(TOKENS // block_rows, block_rows, D)

    def project(block):
        values = block.astype(jnp.float32)
        mean = lax.optimization_barrier(jnp.mean(values, axis=1, keepdims=True))
        centered = values - mean
        var = lax.optimization_barrier(jnp.mean(centered * centered, axis=1, keepdims=True))
        normed = (centered * lax.rsqrt(var + 1e-05) * ln_gain + ln_bias).astype(jnp.bfloat16)
        return jnp.dot(normed, weight, preferred_element_type=jnp.float32).astype(jnp.bfloat16)
    keys = lax.map(project, blocks).reshape(TOKENS, KEYS)
    return (new_master, new_moment1, new_moment2, keys)
```

```python
import functools

import jax
import jax.numpy as jnp
from jax import lax
from jax.experimental import pallas as pl
from jax.experimental.pallas import tpu as pltpu
from jax.sharding import PartitionSpec as P

QBLOCK = 128
MESH = pl.DeviceIdType.MESH
LANES = 512


def expand_rows(values, scales):
    count = values.shape[0]
    blocks = scales.shape[1]
    full = (
        values.astype(jnp.float32).reshape(count, blocks, -1)
        * scales.astype(jnp.float32)[:, :, None]
    )
    return full.reshape(count, -1).astype(jnp.bfloat16)


def shards(tokens, ln_gain, ln_bias, master, grad, moment1, moment2):
    gradient = grad.astype(jnp.float32)
    new_moment1 = 0.9 * moment1 + 0.1 * gradient
    new_moment2 = 0.95 * moment2 + 0.05 * gradient * gradient
    step_size = new_moment1 / 0.19 / (jnp.sqrt(new_moment2 / 0.0975) + 1e-08)
    new_master = master - 0.008 * (step_size + 0.1 * master)
    own_rows, width = new_master.shape
    blocked = new_master.reshape(own_rows, width // QBLOCK, QBLOCK)
    scale = ((jnp.max(jnp.abs(blocked), axis=2) + 1e-06) / 127.0).astype(jnp.bfloat16)
    quant = (
        (blocked / scale.astype(jnp.float32)[:, :, None])
        .astype(jnp.bfloat16)
        .reshape(own_rows, width)
    )
    values = tokens.astype(jnp.float32)
    mean = jnp.mean(values, axis=1, keepdims=True)
    centered = values - mean
    var = jnp.mean(centered * centered, axis=1, keepdims=True)
    normed = (centered * lax.rsqrt(var + 1e-05) * ln_gain + ln_bias).astype(jnp.bfloat16)
    group_values, group_scales = (
        lax.all_gather(quant, "grp", axis=0, tiled=True),
        lax.all_gather(scale, "grp", axis=0, tiled=True),
    )
    weight_rows = expand_rows(group_values, group_scales)
    gathered = lax.all_to_all(normed, "ing", split_axis=1, concat_axis=0, tiled=True)
    summed = lax.psum_scatter(
        jnp.dot(gathered, weight_rows, preferred_element_type=jnp.float32),
        "ing",
        scatter_dimension=0,
        tiled=True,
    )
    result = summed.astype(jnp.bfloat16)
    return (new_master, new_moment1, new_moment2, result)


def adam_kernel(master, grad, moment1, moment2, out_master, out_m1, out_m2, weight):
    gradient = grad[...].astype(jnp.float32)
    old = master[...]
    first = 0.9 * moment1[...] + 0.1 * gradient
    second = 0.95 * moment2[...] + 0.05 * gradient * gradient
    step_size = first / 0.19 / (jnp.sqrt(second / 0.0975) + 1e-08)
    updated = old - 0.008 * (step_size + 0.1 * old)
    out_master[...] = updated
    out_m1[...] = first
    out_m2[...] = second
    largest = jnp.max(jnp.abs(updated), axis=1, keepdims=True)
    scale = ((largest + 1e-06) / 127.0).astype(jnp.bfloat16).astype(jnp.float32)
    quant = (updated / scale).astype(jnp.bfloat16)
    weight[...] = (quant.astype(jnp.float32) * scale).astype(jnp.bfloat16)


def adam(master, grad, moment1, moment2):
    rows, width = master.shape
    block = pl.BlockSpec((rows, QBLOCK), lambda i: (0, i))
    wide = jax.ShapeDtypeStruct((rows, width), jnp.float32)
    return pl.pallas_call(
        adam_kernel,
        grid=(width // QBLOCK,),
        in_specs=[block] * 4,
        out_specs=[block] * 4,
        out_shape=[wide, wide, wide, jax.ShapeDtypeStruct((rows, width), jnp.bfloat16)],
        compiler_params=pltpu.CompilerParams(vmem_limit_bytes=32 * 2**20),
    )(master, grad, moment1, moment2)


def gather_kernel(
    grps, rows, planes, cuts,
    weight, tokens, gain, bias, keys,
    full, tok, norm, acc, part,
    local_sem, recv_sem, send_sem, side_recv, side_send,
):
    cut_c, cut_a, cut_b = cuts
    g = lax.axis_index("grp")
    i = lax.axis_index("ing")
    z, k = i // 2, i % 2
    gx, gy = g + 1 - 2 * (g % 2), lax.rem(g + 2, 4)
    gxy = gy + 1 - 2 * (gy % 2)
    half = 4 * rows
    plane = 2 * half
    window = (half + 127) // 128 * 128
    shift = plane - window
    count, features = tokens.shape
    top = planes - 1

    fetch_w = pltpu.make_async_copy(
        weight, full.at[pl.ds(pl.multiple_of((i * 4 + g) * rows, 16), rows), :], local_sem.at[0])
    fetch_w.start()
    fetch_t = pltpu.make_async_copy(tokens, tok, local_sem.at[1])
    fetch_t.start()

    barrier = pltpu.get_barrier_semaphore()
    for peer in ((gx, i), (gy, i), (g, i + 1 - 2 * k)):
        pl.semaphore_signal(barrier, inc=1, device_id=peer, device_id_type=MESH)

    @pl.when(z < top)
    def _():
        pl.semaphore_signal(barrier, inc=1, device_id=(g, i + 2), device_id_type=MESH)

    @pl.when(z > 0)
    def _():
        pl.semaphore_signal(barrier, inc=1, device_id=(g, i - 2), device_id_type=MESH)

    gap = window - half
    if gap:
        for p in range(planes):
            at = pl.multiple_of(p * plane + half - gap * k, 16)
            full[pl.ds(at, gap), :] = jnp.zeros((gap, full.shape[1]), full.dtype)

    fetch_w.wait()
    pl.semaphore_wait(barrier, 5 - jnp.where(z == top, 1, 0) - jnp.where(z == 0, 1, 0))

    def rows_of(zo, go, lo, hi):
        start = ((zo * 2 + k) * 4 + go) * rows + lo
        return full.at[pl.ds(pl.multiple_of(start, 16), hi - lo), :]

    def copy(kind, zo, go, lo, hi, peer, sent):
        ref = rows_of(zo, go, lo, hi)
        return pltpu.make_async_remote_copy(
            src_ref=ref, dst_ref=ref,
            send_sem=send_sem.at[sent, zo], recv_sem=recv_sem.at[kind, zo],
            device_id=peer, device_id_type=MESH)

    me = (g, i)
    px, py = (gx, i), (gy, i)
    first_c, first_d = (0, cut_c), (cut_b, rows)
    spans = {0: (0, rows), 1: first_c, 2: first_d}

    def along(kind, zo, go, up):
        lo, hi = spans[kind]
        return copy(kind, zo, go, lo, hi, (g, i + 2 if up else i - 2), kind if up else 7 + kind)

    col = {0: g, 1: gx, 2: gy}

    def spread(kind, do):
        @pl.when(z < top)
        def _():
            do(along(kind, z, col[kind], True))

        @pl.when(z > 0)
        def _():
            do(along(kind, z, col[kind], False))

    def forward(kind, zo, do):
        @pl.when((zo < z) & (z < top))
        def _():
            do(along(kind, zo, col[kind], True))

        @pl.when((zo > z) & (z > 0))
        def _():
            do(along(kind, zo, col[kind], False))

    start = lambda c: c.start()
    wait_send = lambda c: c.wait_send()

    def to_x(zo, own):
        return copy(3, zo, g, 0 if own else cut_c, rows, px, 3)

    def to_y(zo, own):
        return copy(5, zo, g, 0, rows if own else cut_b, py, 5)

    def diag_x(zo):
        return copy(4, zo, gy, cut_a, rows, px, 4)

    def diag_y(zo):
        return copy(6, zo, gx, 0, cut_a, py, 6)

    def got(kind, zo, go, lo, hi):
        copy(kind, zo, go, lo, hi, px, kind).wait_recv()

    spread(0, start)
    to_x(z, True).start()
    to_y(z, True).start()

    fetch_t.wait()
    steps = features // LANES

    def slabs(c):
        x = tok[:, pl.ds(pl.multiple_of(c * LANES, LANES), LANES)].astype(jnp.float32)
        return [x[:, j:j + 128] for j in range(0, LANES, 128)]

    def add_up(c, total):
        for x in slabs(c):
            total = total + x
        return total

    zero = jnp.zeros((count, 128), jnp.float32)
    mean = jnp.sum(lax.fori_loop(0, steps, add_up, zero), axis=1, keepdims=True) / features

    def squares(c, total):
        for x in slabs(c):
            total = total + (x - mean) * (x - mean)
        return total

    var = jnp.sum(lax.fori_loop(0, steps, squares, zero), axis=1, keepdims=True) / features
    inv = lax.rsqrt(var + 1e-05)

    def normalize(c, carry):
        at = pl.ds(pl.multiple_of(c * LANES, LANES), LANES)
        x = tok[:, at].astype(jnp.float32)
        norm[0:count, at] = ((x - mean) * inv * gain[:, at] + bias[:, at]).astype(jnp.bfloat16)
        return carry

    lax.fori_loop(0, steps, normalize, 0)

    other = (g, i + 1 - 2 * k)

    def side(p):
        at = pl.ds(pl.multiple_of(p * plane + shift * (1 - k), 128), window)
        return pltpu.make_async_remote_copy(
            src_ref=norm.at[0:count, at], dst_ref=norm.at[count:2 * count, at],
            send_sem=side_send.at[p], recv_sem=side_recv.at[p],
            device_id=other, device_id_type=MESH)

    def side_in(p):
        at = pl.ds(pl.multiple_of(p * plane + shift * k, 128), window)
        return pltpu.make_async_remote_copy(
            src_ref=norm.at[0:count, at], dst_ref=norm.at[count:2 * count, at],
            send_sem=side_send.at[p], recv_sem=side_recv.at[p],
            device_id=other, device_id_type=MESH)

    for p in range(planes):
        side(p).start()

    def product(zo):
        at = pl.multiple_of(zo * plane + shift * k, 128)
        return jnp.dot(norm[:, pl.ds(at, window)], full[pl.ds(at, window), :],
                       preferred_element_type=jnp.float32)

    def whole_in(zo):
        got(0, zo, g, 0, rows)
        forward(0, zo, start)
        to_x(zo, False).start()
        to_y(zo, False).start()

    def parts_in(zo):
        got(1, zo, gx, *first_c)
        forward(1, zo, start)
        got(2, zo, gy, *first_d)
        forward(2, zo, start)

    def columns_in(zo):
        got(3, zo, gx, cut_c, rows)
        diag_y(zo).start()
        got(5, zo, gy, 0, cut_b)
        diag_x(zo).start()

    def diagonal_in(zo):
        got(4, zo, gxy, cut_a, rows)
        got(6, zo, gxy, 0, cut_a)

    low = z < (planes // 2)

    def nth(t):
        mirror = jnp.where(low, z, top - z)
        pick = jnp.where(t - 1 >= mirror, t, t - 1)
        return jnp.where(low, pick, top - pick)

    got(3, z, gx, 0, rows)
    spread(1, start)
    diag_y(z).start()
    got(5, z, gy, 0, rows)
    spread(2, start)
    diag_x(z).start()

    whole_in(nth(1))
    for p in range(planes):
        side_in(p).wait_recv()
    parts_in(nth(1))
    columns_in(nth(1))
    diagonal_in(z)
    acc[...] = product(z)

    for t in range(2, planes):
        whole_in(nth(t))
        parts_in(nth(t))
        columns_in(nth(t))
        diagonal_in(nth(t - 1))
        acc[...] += product(nth(t - 1))
    diagonal_in(nth(top))
    acc[...] += product(nth(top))

    last = pltpu.make_async_remote_copy(
        src_ref=acc.at[count:2 * count, :], dst_ref=part,
        send_sem=side_send.at[planes], recv_sem=side_recv.at[planes],
        device_id=other, device_id_type=MESH)
    last.start()

    for kind in range(3):
        spread(kind, wait_send)
    to_x(z, True).wait_send()
    to_y(z, True).wait_send()
    diag_x(z).wait_send()
    diag_y(z).wait_send()
    for t in range(1, planes):
        zo = nth(t)
        for kind in range(3):
            forward(kind, zo, wait_send)
        to_x(zo, False).wait_send()
        to_y(zo, False).wait_send()
        diag_x(zo).wait_send()
        diag_y(zo).wait_send()
    for p in range(planes):
        side(p).wait_send()
    last.wait()
    keys[...] = (acc[0:count, :] + part[...]).astype(keys.dtype)


def gathered_keys(weight, tokens, gain, bias, grps, planes):
    rows, width = weight.shape
    count, features = tokens.shape
    unit = 16
    units = rows // unit
    cuts = tuple(unit * ((units * n + 3) // 6) for n in (2, 3, 4))
    anywhere = pl.BlockSpec(memory_space=pl.ANY)
    vmem = pl.BlockSpec(memory_space=pltpu.VMEM)
    return pl.pallas_call(
        functools.partial(gather_kernel, grps, rows, planes, cuts),
        out_shape=jax.ShapeDtypeStruct((count, width), jnp.bfloat16),
        in_specs=[anywhere, anywhere, vmem, vmem],
        out_specs=vmem,
        scratch_shapes=[
            pltpu.VMEM((features, width), jnp.bfloat16),
            pltpu.VMEM((count, features), jnp.bfloat16),
            pltpu.VMEM((2 * count, features), jnp.bfloat16),
            pltpu.VMEM((2 * count, width), jnp.float32),
            pltpu.VMEM((count, width), jnp.float32),
            pltpu.SemaphoreType.DMA((2,)),
            pltpu.SemaphoreType.DMA((7, planes)),
            pltpu.SemaphoreType.DMA((10, planes)),
            pltpu.SemaphoreType.DMA((planes + 1,)),
            pltpu.SemaphoreType.DMA((planes + 1,)),
        ],
        compiler_params=pltpu.CompilerParams(
            collective_id=0, has_side_effects=True, vmem_limit_bytes=48 * 2**20),
        cost_estimate=pl.CostEstimate(
            flops=2 * count * features * width,
            bytes_accessed=2 * count * features + 2 * rows * width,
            transcendentals=0),
    )(weight, tokens, gain.reshape(1, -1), bias.reshape(1, -1))


def kernel_shards(grps, planes, tokens, ln_gain, ln_bias, master, grad, moment1, moment2):
    new_master, new_moment1, new_moment2, weight = adam(master, grad, moment1, moment2)
    keys = gathered_keys(weight, tokens, ln_gain, ln_bias, grps, planes)
    return (new_master, new_moment1, new_moment2, keys)


def solution(mesh):
    grps, members = mesh.shape["grp"], mesh.shape["ing"]

    def body(tokens, ln_gain, ln_bias, master, grad, moment1, moment2):
        rows, width = master.shape
        count, features = tokens.shape
        fits = (
            grps == 4 and members == 8 and rows % 16 == 0 and rows >= 96
            and (8 * rows) % 128 == 0 and width % QBLOCK == 0
            and features % LANES == 0 and count % 16 == 0
        )
        plan = functools.partial(kernel_shards, grps, members // 2) if fits else shards
        return plan(tokens, ln_gain, ln_bias, master, grad, moment1, moment2)

    in_specs = (
        P(("grp", "ing"), None),
        P(),
        P(),
        P(("ing", "grp"), None),
        P(("ing", "grp"), None),
        P(("ing", "grp"), None),
        P(("ing", "grp"), None),
    )
    out_specs = (
        P(("ing", "grp"), None),
        P(("ing", "grp"), None),
        P(("ing", "grp"), None),
        P(("grp", "ing"), None),
    )
    return jax.shard_map(body, mesh=mesh, in_specs=in_specs, out_specs=out_specs, check_vma=False)
```

```python
import functools

import jax
import jax.numpy as jnp
from jax import lax
from jax.experimental import pallas as pl
from jax.experimental.pallas import tpu as pltpu
from jax.sharding import PartitionSpec as P

QBLOCK = 128
MESH = pl.DeviceIdType.MESH
LANES = 512


def expand_rows(values, scales):
    count = values.shape[0]
    blocks = scales.shape[1]
    full = (
        values.astype(jnp.float32).reshape(count, blocks, -1)
        * scales.astype(jnp.float32)[:, :, None]
    )
    return full.reshape(count, -1).astype(jnp.bfloat16)


def shards(tokens, ln_gain, ln_bias, master, grad, moment1, moment2):
    gradient = grad.astype(jnp.float32)
    new_moment1 = 0.9 * moment1 + 0.1 * gradient
    new_moment2 = 0.95 * moment2 + 0.05 * gradient * gradient
    step_size = new_moment1 / 0.19 / (jnp.sqrt(new_moment2 / 0.0975) + 1e-08)
    new_master = master - 0.008 * (step_size + 0.1 * master)
    own_rows, width = new_master.shape
    blocked = new_master.reshape(own_rows, width // QBLOCK, QBLOCK)
    scale = ((jnp.max(jnp.abs(blocked), axis=2) + 1e-06) / 127.0).astype(jnp.bfloat16)
    quant = (
        (blocked / scale.astype(jnp.float32)[:, :, None])
        .astype(jnp.bfloat16)
        .reshape(own_rows, width)
    )
    values = tokens.astype(jnp.float32)
    mean = jnp.mean(values, axis=1, keepdims=True)
    centered = values - mean
    var = jnp.mean(centered * centered, axis=1, keepdims=True)
    normed = (centered * lax.rsqrt(var + 1e-05) * ln_gain + ln_bias).astype(jnp.bfloat16)
    group_values, group_scales = (
        lax.all_gather(quant, "grp", axis=0, tiled=True),
        lax.all_gather(scale, "grp", axis=0, tiled=True),
    )
    weight_rows = expand_rows(group_values, group_scales)
    gathered = lax.all_to_all(normed, "ing", split_axis=1, concat_axis=0, tiled=True)
    summed = lax.psum_scatter(
        jnp.dot(gathered, weight_rows, preferred_element_type=jnp.float32),
        "ing",
        scatter_dimension=0,
        tiled=True,
    )
    result = summed.astype(jnp.bfloat16)
    return (new_master, new_moment1, new_moment2, result)


def adam_kernel(master, grad, moment1, moment2, out_master, out_m1, out_m2, weight):
    gradient = grad[...].astype(jnp.float32)
    old = master[...]
    first = 0.9 * moment1[...] + 0.1 * gradient
    second = 0.95 * moment2[...] + 0.05 * gradient * gradient
    step_size = first / 0.19 / (jnp.sqrt(second / 0.0975) + 1e-08)
    updated = old - 0.008 * (step_size + 0.1 * old)
    out_master[...] = updated
    out_m1[...] = first
    out_m2[...] = second
    largest = jnp.max(jnp.abs(updated), axis=1, keepdims=True)
    scale = ((largest + 1e-06) / 127.0).astype(jnp.bfloat16).astype(jnp.float32)
    quant = (updated / scale).astype(jnp.bfloat16)
    weight[...] = (quant.astype(jnp.float32) * scale).astype(jnp.bfloat16)


def adam(master, grad, moment1, moment2):
    rows, width = master.shape
    block = pl.BlockSpec((rows, QBLOCK), lambda i: (0, i))
    wide = jax.ShapeDtypeStruct((rows, width), jnp.float32)
    return pl.pallas_call(
        adam_kernel,
        grid=(width // QBLOCK,),
        in_specs=[block] * 4,
        out_specs=[block] * 4,
        out_shape=[wide, wide, wide, jax.ShapeDtypeStruct((rows, width), jnp.bfloat16)],
        compiler_params=pltpu.CompilerParams(vmem_limit_bytes=60 * 2**20),
    )(master, grad, moment1, moment2)


def gather_kernel(
    grps, rows, planes, cuts,
    weight, tokens, gain, bias, keys,
    full, tok, norm, acc, part,
    local_sem, recv_sem, send_sem, side_recv, side_send,
):
    cut_c, cut_a, cut_b = cuts
    g = lax.axis_index("grp")
    i = lax.axis_index("ing")
    z, k = i // 2, i % 2
    gx, gy = g + 1 - 2 * (g % 2), lax.rem(g + 2, 4)
    gxy = gy + 1 - 2 * (gy % 2)
    half = 4 * rows
    plane = 2 * half
    window = (half + 127) // 128 * 128
    shift = plane - window
    count, features = tokens.shape
    top = planes - 1

    fetch_w = pltpu.make_async_copy(
        weight, full.at[pl.ds(pl.multiple_of((i * 4 + g) * rows, 16), rows), :], local_sem.at[0])
    fetch_w.start()
    fetch_t = pltpu.make_async_copy(tokens, tok, local_sem.at[1])
    fetch_t.start()

    barrier = pltpu.get_barrier_semaphore()
    for peer in ((gx, i), (gy, i), (g, i + 1 - 2 * k)):
        pl.semaphore_signal(barrier, inc=1, device_id=peer, device_id_type=MESH)

    @pl.when(z < top)
    def _():
        pl.semaphore_signal(barrier, inc=1, device_id=(g, i + 2), device_id_type=MESH)

    @pl.when(z > 0)
    def _():
        pl.semaphore_signal(barrier, inc=1, device_id=(g, i - 2), device_id_type=MESH)

    gap = window - half
    if gap:
        for p in range(planes):
            at = pl.multiple_of(p * plane + half - gap * k, 16)
            full[pl.ds(at, gap), :] = jnp.zeros((gap, full.shape[1]), full.dtype)

    fetch_w.wait()
    pl.semaphore_wait(barrier, 5 - jnp.where(z == top, 1, 0) - jnp.where(z == 0, 1, 0))

    def rows_of(zo, go, lo, hi):
        start = ((zo * 2 + k) * 4 + go) * rows + lo
        return full.at[pl.ds(pl.multiple_of(start, 16), hi - lo), :]

    def copy(kind, zo, go, lo, hi, peer, sent):
        ref = rows_of(zo, go, lo, hi)
        return pltpu.make_async_remote_copy(
            src_ref=ref, dst_ref=ref,
            send_sem=send_sem.at[sent, zo], recv_sem=recv_sem.at[kind, zo],
            device_id=peer, device_id_type=MESH)

    px, py = (gx, i), (gy, i)
    spans = {0: (0, cut_a), 1: (0, cut_c), 2: (cut_b, rows), 3: (cut_a, rows)}
    col = {0: g, 1: gx, 2: gy, 3: g}

    def along(kind, zo, up):
        peer = (g, i + 2 if up else i - 2)
        return copy(kind, zo, col[kind], *spans[kind], peer, kind if up else 10 + kind)

    def spread(kind, do):
        @pl.when(z < top)
        def _():
            do(along(kind, z, True))

        @pl.when(z > 0)
        def _():
            do(along(kind, z, False))

    def forward(kind, zo, do):
        @pl.when((zo < z) & (z < top))
        def _():
            do(along(kind, zo, True))

        @pl.when((zo > z) & (z > 0))
        def _():
            do(along(kind, zo, False))

    start = lambda c: c.start()
    wait_send = lambda c: c.wait_send()

    own_x = [copy(4, z, g, 0, cut_a, px, 4), copy(5, z, g, cut_a, rows, px, 5)]
    own_y = [copy(8, z, g, cut_a, rows, py, 8), copy(7, z, g, 0, cut_a, py, 7)]

    def to_x(zo):
        return copy(4, zo, g, cut_c, rows, px, 4)

    def to_y(zo):
        return copy(7, zo, g, 0, cut_b, py, 7)

    def diag_x(zo):
        return copy(6, zo, gy, cut_a, rows, px, 6)

    def diag_y(zo):
        return copy(9, zo, gx, 0, cut_a, py, 9)

    def got(kind, zo, go, lo, hi):
        copy(kind, zo, go, lo, hi, px, kind).wait_recv()

    spread(0, start)
    own_x[0].start()
    own_y[0].start()
    spread(3, start)
    own_x[1].start()
    own_y[1].start()

    fetch_t.wait()
    steps = features // LANES

    def slabs(c):
        x = tok[:, pl.ds(pl.multiple_of(c * LANES, LANES), LANES)].astype(jnp.float32)
        return [x[:, j:j + 128] for j in range(0, LANES, 128)]

    def add_up(c, total):
        for x in slabs(c):
            total = total + x
        return total

    zero = jnp.zeros((count, 128), jnp.float32)
    mean = jnp.sum(lax.fori_loop(0, steps, add_up, zero), axis=1, keepdims=True) / features

    def squares(c, total):
        for x in slabs(c):
            total = total + (x - mean) * (x - mean)
        return total

    var = jnp.sum(lax.fori_loop(0, steps, squares, zero), axis=1, keepdims=True) / features
    inv = lax.rsqrt(var + 1e-05)

    def normalize(c, carry):
        at = pl.ds(pl.multiple_of(c * LANES, LANES), LANES)
        x = tok[:, at].astype(jnp.float32)
        norm[0:count, at] = ((x - mean) * inv * gain[at][None, :] + bias[at][None, :]).astype(jnp.bfloat16)
        return carry

    lax.fori_loop(0, steps, normalize, 0)

    other = (g, i + 1 - 2 * k)

    def side(p):
        at = pl.ds(pl.multiple_of(p * plane + shift * (1 - k), 128), window)
        return pltpu.make_async_remote_copy(
            src_ref=norm.at[0:count, at], dst_ref=norm.at[count:2 * count, at],
            send_sem=side_send.at[p], recv_sem=side_recv.at[p],
            device_id=other, device_id_type=MESH)

    def side_in(p):
        at = pl.ds(pl.multiple_of(p * plane + shift * k, 128), window)
        return pltpu.make_async_remote_copy(
            src_ref=norm.at[0:count, at], dst_ref=norm.at[count:2 * count, at],
            send_sem=side_send.at[p], recv_sem=side_recv.at[p],
            device_id=other, device_id_type=MESH)

    for p in range(planes):
        side(p).start()

    def product(zo):
        at = pl.multiple_of(zo * plane + shift * k, 128)
        return jnp.dot(norm[:, pl.ds(at, window)], full[pl.ds(at, window), :],
                       preferred_element_type=jnp.float32)

    def whole_in(zo):
        got(0, zo, g, *spans[0])
        forward(0, zo, start)
        got(3, zo, g, *spans[3])
        forward(3, zo, start)
        to_x(zo).start()
        to_y(zo).start()

    def parts_in(zo):
        got(1, zo, gx, *spans[1])
        forward(1, zo, start)
        got(2, zo, gy, *spans[2])
        forward(2, zo, start)

    def columns_in(zo):
        got(4, zo, gx, cut_c, rows)
        diag_y(zo).start()
        got(7, zo, gy, 0, cut_b)
        diag_x(zo).start()

    def diagonal_in(zo):
        got(6, zo, gxy, cut_a, rows)
        got(9, zo, gxy, 0, cut_a)

    low = z < (planes // 2)

    def nth(t):
        mirror = jnp.where(low, z, top - z)
        pick = jnp.where(t - 1 >= mirror, t, t - 1)
        return jnp.where(low, pick, top - pick)

    end = (z == 0) | (z == top)
    got(4, z, gx, 0, cut_a)
    diag_y(z).start()
    got(8, z, gy, cut_a, rows)
    diag_x(z).start()
    whole_in(nth(1))

    @pl.when(end)
    def _():
        spread(1, start)
        spread(2, start)

    for p in range(planes):
        side_in(p).wait_recv()
    for t in range(2, top):
        whole_in(nth(t))
    got(5, z, gx, cut_a, rows)
    got(7, z, gy, 0, cut_a)
    diagonal_in(z)
    acc[...] = product(z)
    whole_in(nth(top))

    @pl.when(jnp.logical_not(end))
    def _():
        spread(1, start)
        spread(2, start)

    for t in range(1, planes):
        parts_in(nth(t))
        columns_in(nth(t))
        if t > 1:
            diagonal_in(nth(t - 1))
            acc[...] += product(nth(t - 1))
    diagonal_in(nth(top))
    acc[...] += product(nth(top))

    last = pltpu.make_async_remote_copy(
        src_ref=acc.at[count:2 * count, :], dst_ref=part,
        send_sem=side_send.at[planes], recv_sem=side_recv.at[planes],
        device_id=other, device_id_type=MESH)
    last.start()

    for kind in range(4):
        spread(kind, wait_send)
    for c in own_x + own_y + [diag_x(z), diag_y(z)]:
        c.wait_send()
    for t in range(1, planes):
        zo = nth(t)
        for kind in range(4):
            forward(kind, zo, wait_send)
        for c in (to_x(zo), to_y(zo), diag_x(zo), diag_y(zo)):
            c.wait_send()
    for p in range(planes):
        side(p).wait_send()
    last.wait()
    keys[...] = (acc[0:count, :] + part[...]).astype(keys.dtype)


def gathered_keys(weight, tokens, gain, bias, grps, planes):
    rows, width = weight.shape
    count, features = tokens.shape
    unit = 16
    units = rows // unit
    edge = units // 3
    cuts = (unit * edge, unit * ((units + 1) // 2), unit * (units - edge))
    anywhere = pl.BlockSpec(memory_space=pl.ANY)
    vmem = pl.BlockSpec(memory_space=pltpu.VMEM)
    return pl.pallas_call(
        functools.partial(gather_kernel, grps, rows, planes, cuts),
        out_shape=jax.ShapeDtypeStruct((count, width), jnp.bfloat16),
        in_specs=[anywhere, anywhere, vmem, vmem],
        out_specs=vmem,
        scratch_shapes=[
            pltpu.VMEM((features, width), jnp.bfloat16),
            pltpu.VMEM((count, features), jnp.bfloat16),
            pltpu.VMEM((2 * count, features), jnp.bfloat16),
            pltpu.VMEM((2 * count, width), jnp.float32),
            pltpu.VMEM((count, width), jnp.float32),
            pltpu.SemaphoreType.DMA((2,)),
            pltpu.SemaphoreType.DMA((10, planes)),
            pltpu.SemaphoreType.DMA((14, planes)),
            pltpu.SemaphoreType.DMA((planes + 1,)),
            pltpu.SemaphoreType.DMA((planes + 1,)),
        ],
        compiler_params=pltpu.CompilerParams(
            collective_id=0, has_side_effects=True, vmem_limit_bytes=60 * 2**20),
        cost_estimate=pl.CostEstimate(
            flops=2 * count * features * width,
            bytes_accessed=2 * count * features + 2 * rows * width,
            transcendentals=0),
    )(weight, tokens, gain, bias)


def kernel_shards(grps, planes, tokens, ln_gain, ln_bias, master, grad, moment1, moment2):
    new_master, new_moment1, new_moment2, weight = adam(master, grad, moment1, moment2)
    keys = gathered_keys(weight, tokens, ln_gain, ln_bias, grps, planes)
    return (new_master, new_moment1, new_moment2, keys)


def solution(mesh):
    grps, members = mesh.shape["grp"], mesh.shape["ing"]

    def body(tokens, ln_gain, ln_bias, master, grad, moment1, moment2):
        rows, width = master.shape
        count, features = tokens.shape
        fits = (
            grps == 4 and members == 8 and rows % 16 == 0 and rows >= 96
            and (8 * rows) % 128 == 0 and width % QBLOCK == 0
            and features % LANES == 0 and count % 16 == 0
        )
        plan = functools.partial(kernel_shards, grps, members // 2) if fits else shards
        return plan(tokens, ln_gain, ln_bias, master, grad, moment1, moment2)

    in_specs = (
        P(("grp", "ing"), None),
        P(),
        P(),
        P(("ing", "grp"), None),
        P(("ing", "grp"), None),
        P(("ing", "grp"), None),
        P(("ing", "grp"), None),
    )
    out_specs = (
        P(("ing", "grp"), None),
        P(("ing", "grp"), None),
        P(("ing", "grp"), None),
        P(("grp", "ing"), None),
    )
    return jax.shard_map(body, mesh=mesh, in_specs=in_specs, out_specs=out_specs, check_vma=False)
```

```python
import functools

import jax
import jax.numpy as jnp
from jax import lax
from jax.experimental import pallas as pl
from jax.experimental.pallas import tpu as pltpu
from jax.sharding import PartitionSpec as P

QBLOCK = 128
MESH = pl.DeviceIdType.MESH
LANES = 512


def expand_rows(values, scales):
    count = values.shape[0]
    blocks = scales.shape[1]
    full = (
        values.astype(jnp.float32).reshape(count, blocks, -1)
        * scales.astype(jnp.float32)[:, :, None]
    )
    return full.reshape(count, -1).astype(jnp.bfloat16)


def shards(tokens, ln_gain, ln_bias, master, grad, moment1, moment2):
    gradient = grad.astype(jnp.float32)
    new_moment1 = 0.9 * moment1 + 0.1 * gradient
    new_moment2 = 0.95 * moment2 + 0.05 * gradient * gradient
    step_size = new_moment1 / 0.19 / (jnp.sqrt(new_moment2 / 0.0975) + 1e-08)
    new_master = master - 0.008 * (step_size + 0.1 * master)
    own_rows, width = new_master.shape
    blocked = new_master.reshape(own_rows, width // QBLOCK, QBLOCK)
    scale = ((jnp.max(jnp.abs(blocked), axis=2) + 1e-06) / 127.0).astype(jnp.bfloat16)
    quant = (
        (blocked / scale.astype(jnp.float32)[:, :, None])
        .astype(jnp.bfloat16)
        .reshape(own_rows, width)
    )
    values = tokens.astype(jnp.float32)
    mean = jnp.mean(values, axis=1, keepdims=True)
    centered = values - mean
    var = jnp.mean(centered * centered, axis=1, keepdims=True)
    normed = (centered * lax.rsqrt(var + 1e-05) * ln_gain + ln_bias).astype(jnp.bfloat16)
    group_values, group_scales = (
        lax.all_gather(quant, "grp", axis=0, tiled=True),
        lax.all_gather(scale, "grp", axis=0, tiled=True),
    )
    weight_rows = expand_rows(group_values, group_scales)
    gathered = lax.all_to_all(normed, "ing", split_axis=1, concat_axis=0, tiled=True)
    summed = lax.psum_scatter(
        jnp.dot(gathered, weight_rows, preferred_element_type=jnp.float32),
        "ing",
        scatter_dimension=0,
        tiled=True,
    )
    result = summed.astype(jnp.bfloat16)
    return (new_master, new_moment1, new_moment2, result)


def adam_kernel(master, grad, moment1, moment2, out_master, out_m1, out_m2, weight):
    gradient = grad[...].astype(jnp.float32)
    old = master[...]
    first = 0.9 * moment1[...] + 0.1 * gradient
    second = 0.95 * moment2[...] + 0.05 * gradient * gradient
    step_size = first * (1 / 0.19) / (jnp.sqrt(second * (1 / 0.0975)) + 1e-08)
    updated = old - 0.008 * (step_size + 0.1 * old)
    out_master[...] = updated
    out_m1[...] = first
    out_m2[...] = second
    for lo in range(0, updated.shape[1], QBLOCK):
        block = updated[:, lo:lo + QBLOCK]
        largest = jnp.max(jnp.abs(block), axis=1, keepdims=True)
        scale = ((largest + 1e-06) / 127.0).astype(jnp.bfloat16).astype(jnp.float32)
        quant = (block * (1.0 / scale)).astype(jnp.bfloat16)
        weight[:, lo:lo + QBLOCK] = (quant.astype(jnp.float32) * scale).astype(jnp.bfloat16)


def adam(master, grad, moment1, moment2):
    rows, width = master.shape
    block = pl.BlockSpec((rows, 2 * QBLOCK), lambda i: (0, i))
    wide = jax.ShapeDtypeStruct((rows, width), jnp.float32)
    return pl.pallas_call(
        adam_kernel,
        grid=(width // (2 * QBLOCK),),
        in_specs=[block] * 4,
        out_specs=[block] * 4,
        out_shape=[wide, wide, wide, jax.ShapeDtypeStruct((rows, width), jnp.bfloat16)],
        compiler_params=pltpu.CompilerParams(vmem_limit_bytes=60 * 2**20),
    )(master, grad, moment1, moment2)


def gather_kernel(
    grps, rows, planes, cuts,
    weight, tokens, gain, bias, keys,
    full, tok, norm, acc, part,
    local_sem, recv_sem, send_sem, side_recv, side_send,
):
    cut_c, cut_a, cut_b = cuts
    g = lax.axis_index("grp")
    i = lax.axis_index("ing")
    z, k = i // 2, i % 2
    gx, gy = g + 1 - 2 * (g % 2), lax.rem(g + 2, 4)
    gxy = gy + 1 - 2 * (gy % 2)
    half = 4 * rows
    plane = 2 * half
    window = (half + 127) // 128 * 128
    shift = plane - window
    count, features = tokens.shape
    top = planes - 1

    fetch_w = pltpu.make_async_copy(
        weight, full.at[pl.ds(pl.multiple_of((i * 4 + g) * rows, 16), rows), :], local_sem.at[0])
    fetch_w.start()
    fetch_t = pltpu.make_async_copy(tokens, tok, local_sem.at[1])
    fetch_t.start()

    barrier = pltpu.get_barrier_semaphore()
    for peer in ((gx, i), (gy, i), (g, i + 1 - 2 * k)):
        pl.semaphore_signal(barrier, inc=1, device_id=peer, device_id_type=MESH)

    @pl.when(z < top)
    def _():
        pl.semaphore_signal(barrier, inc=1, device_id=(g, i + 2), device_id_type=MESH)

    @pl.when(z > 0)
    def _():
        pl.semaphore_signal(barrier, inc=1, device_id=(g, i - 2), device_id_type=MESH)

    gap = window - half
    if gap:
        for p in range(planes):
            at = pl.multiple_of(p * plane + half - gap * k, 16)
            full[pl.ds(at, gap), :] = jnp.zeros((gap, full.shape[1]), full.dtype)

    fetch_w.wait()
    pl.semaphore_wait(barrier, 5 - jnp.where(z == top, 1, 0) - jnp.where(z == 0, 1, 0))

    def rows_of(zo, go, lo, hi):
        start = ((zo * 2 + k) * 4 + go) * rows + lo
        return full.at[pl.ds(pl.multiple_of(start, 16), hi - lo), :]

    def copy(kind, zo, go, lo, hi, peer, sent):
        ref = rows_of(zo, go, lo, hi)
        return pltpu.make_async_remote_copy(
            src_ref=ref, dst_ref=ref,
            send_sem=send_sem.at[sent, zo], recv_sem=recv_sem.at[kind, zo],
            device_id=peer, device_id_type=MESH)

    px, py = (gx, i), (gy, i)
    spans = {0: (0, cut_a), 1: (0, cut_c), 2: (cut_b, rows), 3: (cut_a, rows)}
    col = {0: g, 1: gx, 2: gy, 3: g}

    def along(kind, zo, up):
        peer = (g, i + 2 if up else i - 2)
        return copy(kind, zo, col[kind], *spans[kind], peer, kind if up else 12 + kind)

    def spread(kind, do):
        @pl.when(z < top)
        def _():
            do(along(kind, z, True))

        @pl.when(z > 0)
        def _():
            do(along(kind, z, False))

    def forward(kind, zo, do):
        @pl.when((zo < z) & (z < top))
        def _():
            do(along(kind, zo, True))

        @pl.when((zo > z) & (z > 0))
        def _():
            do(along(kind, zo, False))

    start = lambda c: c.start()
    wait_send = lambda c: c.wait_send()

    own_x = [copy(4, z, g, 0, cut_a, px, 4), copy(5, z, g, cut_a, rows, px, 5)]
    own_y = [copy(8, z, g, cut_a, rows, py, 8), copy(7, z, g, 0, cut_a, py, 7)]

    def to_x(zo):
        return copy(4, zo, g, cut_c, rows, px, 4)

    def to_y(zo):
        return copy(7, zo, g, 0, cut_b, py, 7)

    own_diag = [copy(9, z, gx, 0, cut_a, py, 9), copy(6, z, gy, cut_a, rows, px, 6)]

    def part_c(zo):
        return copy(9, zo, gx, 0, cut_c, py, 9)

    def part_a(zo):
        return copy(11, zo, gx, cut_c, cut_a, py, 11)

    def part_b(zo):
        return copy(10, zo, gy, cut_a, cut_b, px, 10)

    def part_d(zo):
        return copy(6, zo, gy, cut_b, rows, px, 6)

    def got(kind, zo, go, lo, hi):
        copy(kind, zo, go, lo, hi, px, kind).wait_recv()

    spread(0, start)
    own_x[0].start()
    own_y[0].start()
    spread(3, start)
    own_x[1].start()
    own_y[1].start()

    fetch_t.wait()
    steps = features // LANES

    def slabs(c):
        x = tok[:, pl.ds(pl.multiple_of(c * LANES, LANES), LANES)].astype(jnp.float32)
        return [x[:, j:j + 128] for j in range(0, LANES, 128)]

    def add_up(c, total):
        for x in slabs(c):
            total = total + x
        return total

    zero = jnp.zeros((count, 128), jnp.float32)
    mean = jnp.sum(lax.fori_loop(0, steps, add_up, zero), axis=1, keepdims=True) / features

    def squares(c, total):
        for x in slabs(c):
            total = total + (x - mean) * (x - mean)
        return total

    var = jnp.sum(lax.fori_loop(0, steps, squares, zero), axis=1, keepdims=True) / features
    inv = lax.rsqrt(var + 1e-05)

    def normalize(c, carry):
        at = pl.ds(pl.multiple_of(c * LANES, LANES), LANES)
        x = tok[:, at].astype(jnp.float32)
        norm[0:count, at] = ((x - mean) * inv * gain[at][None, :] + bias[at][None, :]).astype(jnp.bfloat16)
        return carry

    lax.fori_loop(0, steps, normalize, 0)

    other = (g, i + 1 - 2 * k)

    def side(p):
        at = pl.ds(pl.multiple_of(p * plane + shift * (1 - k), 128), window)
        return pltpu.make_async_remote_copy(
            src_ref=norm.at[0:count, at], dst_ref=norm.at[count:2 * count, at],
            send_sem=side_send.at[p], recv_sem=side_recv.at[p],
            device_id=other, device_id_type=MESH)

    def side_in(p):
        at = pl.ds(pl.multiple_of(p * plane + shift * k, 128), window)
        return pltpu.make_async_remote_copy(
            src_ref=norm.at[0:count, at], dst_ref=norm.at[count:2 * count, at],
            send_sem=side_send.at[p], recv_sem=side_recv.at[p],
            device_id=other, device_id_type=MESH)

    for p in range(planes):
        side(p).start()

    def product(zo):
        at = pl.multiple_of(zo * plane + shift * k, 128)
        return jnp.dot(norm[:, pl.ds(at, window)], full[pl.ds(at, window), :],
                       preferred_element_type=jnp.float32)

    def whole_in(zo):
        got(0, zo, g, *spans[0])
        forward(0, zo, start)
        got(3, zo, g, *spans[3])
        forward(3, zo, start)
        to_x(zo).start()
        to_y(zo).start()

    def parts_in(zo):
        got(1, zo, gx, *spans[1])
        forward(1, zo, start)
        part_c(zo).start()
        got(2, zo, gy, *spans[2])
        forward(2, zo, start)
        part_d(zo).start()

    def columns_in(zo):
        got(4, zo, gx, cut_c, rows)
        part_a(zo).start()
        got(7, zo, gy, 0, cut_b)
        part_b(zo).start()

    def diagonal_in(zo):
        got(10, zo, gxy, cut_a, cut_b)
        got(11, zo, gxy, cut_c, cut_a)
        got(6, zo, gxy, cut_b, rows)
        got(9, zo, gxy, 0, cut_c)

    low = z < (planes // 2)

    def nth(t):
        mirror = jnp.where(low, z, top - z)
        pick = jnp.where(t - 1 >= mirror, t, t - 1)
        return jnp.where(low, pick, top - pick)

    end = (z == 0) | (z == top)
    got(4, z, gx, 0, cut_a)
    own_diag[0].start()
    got(8, z, gy, cut_a, rows)
    own_diag[1].start()
    whole_in(nth(1))

    @pl.when(end)
    def _():
        spread(1, start)
        spread(2, start)

    for p in range(planes):
        side_in(p).wait_recv()
    for t in range(2, top):
        whole_in(nth(t))
    got(5, z, gx, cut_a, rows)
    got(7, z, gy, 0, cut_a)
    got(6, z, gxy, cut_a, rows)
    got(9, z, gxy, 0, cut_a)
    acc[...] = product(z)
    whole_in(nth(top))

    @pl.when(jnp.logical_not(end))
    def _():
        spread(1, start)
        spread(2, start)

    for t in range(1, planes):
        columns_in(nth(t))
        parts_in(nth(t))
        if t > 1:
            diagonal_in(nth(t - 1))
            acc[...] += product(nth(t - 1))
    diagonal_in(nth(top))
    acc[...] += product(nth(top))

    last = pltpu.make_async_remote_copy(
        src_ref=acc.at[count:2 * count, :], dst_ref=part,
        send_sem=side_send.at[planes], recv_sem=side_recv.at[planes],
        device_id=other, device_id_type=MESH)
    last.start()

    for kind in range(4):
        spread(kind, wait_send)
    for c in own_x + own_y + own_diag:
        c.wait_send()
    for t in range(1, planes):
        zo = nth(t)
        for kind in range(4):
            forward(kind, zo, wait_send)
        for c in (to_x(zo), to_y(zo), part_a(zo), part_b(zo), part_c(zo), part_d(zo)):
            c.wait_send()
    for p in range(planes):
        side(p).wait_send()
    last.wait()
    keys[...] = (acc[0:count, :] + part[...]).astype(keys.dtype)


def gathered_keys(weight, tokens, gain, bias, grps, planes):
    rows, width = weight.shape
    count, features = tokens.shape
    unit = 16
    units = rows // unit
    edge = units // 3
    cuts = (unit * edge, unit * ((units + 1) // 2), unit * (units - edge))
    anywhere = pl.BlockSpec(memory_space=pl.ANY)
    vmem = pl.BlockSpec(memory_space=pltpu.VMEM)
    return pl.pallas_call(
        functools.partial(gather_kernel, grps, rows, planes, cuts),
        out_shape=jax.ShapeDtypeStruct((count, width), jnp.bfloat16),
        in_specs=[anywhere, anywhere, vmem, vmem],
        out_specs=vmem,
        scratch_shapes=[
            pltpu.VMEM((features, width), jnp.bfloat16),
            pltpu.VMEM((count, features), jnp.bfloat16),
            pltpu.VMEM((2 * count, features), jnp.bfloat16),
            pltpu.VMEM((2 * count, width), jnp.float32),
            pltpu.VMEM((count, width), jnp.float32),
            pltpu.SemaphoreType.DMA((2,)),
            pltpu.SemaphoreType.DMA((12, planes)),
            pltpu.SemaphoreType.DMA((16, planes)),
            pltpu.SemaphoreType.DMA((planes + 1,)),
            pltpu.SemaphoreType.DMA((planes + 1,)),
        ],
        compiler_params=pltpu.CompilerParams(
            collective_id=0, has_side_effects=True, vmem_limit_bytes=60 * 2**20),
        cost_estimate=pl.CostEstimate(
            flops=2 * count * features * width,
            bytes_accessed=2 * count * features + 2 * rows * width,
            transcendentals=0),
    )(weight, tokens, gain, bias)


def kernel_shards(grps, planes, tokens, ln_gain, ln_bias, master, grad, moment1, moment2):
    new_master, new_moment1, new_moment2, weight = adam(master, grad, moment1, moment2)
    keys = gathered_keys(weight, tokens, ln_gain, ln_bias, grps, planes)
    return (new_master, new_moment1, new_moment2, keys)


def solution(mesh):
    grps, members = mesh.shape["grp"], mesh.shape["ing"]

    def body(tokens, ln_gain, ln_bias, master, grad, moment1, moment2):
        rows, width = master.shape
        count, features = tokens.shape
        fits = (
            grps == 4 and members == 8 and rows % 16 == 0 and rows >= 96
            and (8 * rows) % 128 == 0 and width % QBLOCK == 0
            and features % LANES == 0 and count % 16 == 0
        )
        plan = functools.partial(kernel_shards, grps, members // 2) if fits else shards
        return plan(tokens, ln_gain, ln_bias, master, grad, moment1, moment2)

    in_specs = (
        P(("grp", "ing"), None),
        P(),
        P(),
        P(("ing", "grp"), None),
        P(("ing", "grp"), None),
        P(("ing", "grp"), None),
        P(("ing", "grp"), None),
    )
    out_specs = (
        P(("ing", "grp"), None),
        P(("ing", "grp"), None),
        P(("ing", "grp"), None),
        P(("grp", "ing"), None),
    )
    return jax.shard_map(body, mesh=mesh, in_specs=in_specs, out_specs=out_specs, check_vma=False)
```

```python
import functools

import jax
import jax.numpy as jnp
from jax import lax
from jax.experimental import pallas as pl
from jax.experimental.pallas import tpu as pltpu
from jax.sharding import PartitionSpec as P

QBLOCK = 128
MESH = pl.DeviceIdType.MESH
LANES = 512


def expand_rows(values, scales):
    count = values.shape[0]
    blocks = scales.shape[1]
    full = (
        values.astype(jnp.float32).reshape(count, blocks, -1)
        * scales.astype(jnp.float32)[:, :, None]
    )
    return full.reshape(count, -1).astype(jnp.bfloat16)


def shards(tokens, ln_gain, ln_bias, master, grad, moment1, moment2):
    gradient = grad.astype(jnp.float32)
    new_moment1 = 0.9 * moment1 + 0.1 * gradient
    new_moment2 = 0.95 * moment2 + 0.05 * gradient * gradient
    step_size = new_moment1 / 0.19 / (jnp.sqrt(new_moment2 / 0.0975) + 1e-08)
    new_master = master - 0.008 * (step_size + 0.1 * master)
    own_rows, width = new_master.shape
    blocked = new_master.reshape(own_rows, width // QBLOCK, QBLOCK)
    scale = ((jnp.max(jnp.abs(blocked), axis=2) + 1e-06) / 127.0).astype(jnp.bfloat16)
    quant = (
        (blocked / scale.astype(jnp.float32)[:, :, None])
        .astype(jnp.bfloat16)
        .reshape(own_rows, width)
    )
    values = tokens.astype(jnp.float32)
    mean = jnp.mean(values, axis=1, keepdims=True)
    centered = values - mean
    var = jnp.mean(centered * centered, axis=1, keepdims=True)
    normed = (centered * lax.rsqrt(var + 1e-05) * ln_gain + ln_bias).astype(jnp.bfloat16)
    group_values, group_scales = (
        lax.all_gather(quant, "grp", axis=0, tiled=True),
        lax.all_gather(scale, "grp", axis=0, tiled=True),
    )
    weight_rows = expand_rows(group_values, group_scales)
    gathered = lax.all_to_all(normed, "ing", split_axis=1, concat_axis=0, tiled=True)
    summed = lax.psum_scatter(
        jnp.dot(gathered, weight_rows, preferred_element_type=jnp.float32),
        "ing",
        scatter_dimension=0,
        tiled=True,
    )
    result = summed.astype(jnp.bfloat16)
    return (new_master, new_moment1, new_moment2, result)


def adam_kernel(master, grad, moment1, moment2, out_master, out_m1, out_m2, weight):
    gradient = grad[...].astype(jnp.float32)
    old = master[...]
    first = 0.9 * moment1[...] + 0.1 * gradient
    second = 0.95 * moment2[...] + 0.05 * gradient * gradient
    step_size = first * (1 / 0.19) / (jnp.sqrt(second * (1 / 0.0975)) + 1e-08)
    updated = old - 0.008 * (step_size + 0.1 * old)
    out_master[...] = updated
    out_m1[...] = first
    out_m2[...] = second
    for lo in range(0, updated.shape[1], QBLOCK):
        block = updated[:, lo:lo + QBLOCK]
        largest = jnp.max(jnp.abs(block), axis=1, keepdims=True)
        scale = ((largest + 1e-06) / 127.0).astype(jnp.bfloat16).astype(jnp.float32)
        quant = (block * (1.0 / scale)).astype(jnp.bfloat16)
        weight[:, lo:lo + QBLOCK] = (quant.astype(jnp.float32) * scale).astype(jnp.bfloat16)


def adam(master, grad, moment1, moment2):
    rows, width = master.shape
    block = pl.BlockSpec((rows, 2 * QBLOCK), lambda i: (0, i))
    wide = jax.ShapeDtypeStruct((rows, width), jnp.float32)
    return pl.pallas_call(
        adam_kernel,
        grid=(width // (2 * QBLOCK),),
        in_specs=[block] * 4,
        out_specs=[block] * 4,
        out_shape=[wide, wide, wide, jax.ShapeDtypeStruct((rows, width), jnp.bfloat16)],
        compiler_params=pltpu.CompilerParams(vmem_limit_bytes=60 * 2**20),
    )(master, grad, moment1, moment2)


def gather_kernel(
    grps, rows, planes, cuts,
    weight, tokens, gain, bias, keys,
    full, tok, norm, acc, part,
    local_sem, recv_sem, send_sem, side_recv, side_send,
):
    cut_c, cut_a, cut_b = cuts
    g = lax.axis_index("grp")
    i = lax.axis_index("ing")
    z, k = i // 2, i % 2
    gx, gy = g + 1 - 2 * (g % 2), lax.rem(g + 2, 4)
    gxy = gy + 1 - 2 * (gy % 2)
    half = 4 * rows
    plane = 2 * half
    window = (half + 127) // 128 * 128
    shift = plane - window
    count, features = tokens.shape
    top = planes - 1

    fetch_w = pltpu.make_async_copy(
        weight, full.at[pl.ds(pl.multiple_of((i * 4 + g) * rows, 16), rows), :], local_sem.at[0])
    fetch_w.start()
    fetch_t = pltpu.make_async_copy(tokens, tok, local_sem.at[1])
    fetch_t.start()

    barrier = pltpu.get_barrier_semaphore()
    for peer in ((gx, i), (gy, i), (g, i + 1 - 2 * k)):
        pl.semaphore_signal(barrier, inc=1, device_id=peer, device_id_type=MESH)

    @pl.when(z < top)
    def _():
        pl.semaphore_signal(barrier, inc=1, device_id=(g, i + 2), device_id_type=MESH)

    @pl.when(z > 0)
    def _():
        pl.semaphore_signal(barrier, inc=1, device_id=(g, i - 2), device_id_type=MESH)

    gap = window - half
    if gap:
        for p in range(planes):
            at = pl.multiple_of(p * plane + half - gap * k, 16)
            full[pl.ds(at, gap), :] = jnp.zeros((gap, full.shape[1]), full.dtype)

    fetch_w.wait()
    pl.semaphore_wait(barrier, 5 - jnp.where(z == top, 1, 0) - jnp.where(z == 0, 1, 0))

    def rows_of(zo, go, lo, hi):
        start = ((zo * 2 + k) * 4 + go) * rows + lo
        return full.at[pl.ds(pl.multiple_of(start, 16), hi - lo), :]

    def copy(kind, zo, go, lo, hi, peer, sent):
        ref = rows_of(zo, go, lo, hi)
        return pltpu.make_async_remote_copy(
            src_ref=ref, dst_ref=ref,
            send_sem=send_sem.at[sent, zo], recv_sem=recv_sem.at[kind, zo],
            device_id=peer, device_id_type=MESH)

    px, py = (gx, i), (gy, i)
    spans = {0: (0, cut_a), 1: (0, cut_c), 2: (cut_b, rows), 3: (cut_a, rows)}
    col = {0: g, 1: gx, 2: gy, 3: g}

    def along(kind, zo, up):
        peer = (g, i + 2 if up else i - 2)
        return copy(kind, zo, col[kind], *spans[kind], peer, kind if up else 12 + kind)

    def spread(kind, do):
        @pl.when(z < top)
        def _():
            do(along(kind, z, True))

        @pl.when(z > 0)
        def _():
            do(along(kind, z, False))

    def forward(kind, zo, do):
        @pl.when((zo < z) & (z < top))
        def _():
            do(along(kind, zo, True))

        @pl.when((zo > z) & (z > 0))
        def _():
            do(along(kind, zo, False))

    start = lambda c: c.start()
    wait_send = lambda c: c.wait_send()

    own_x = [copy(4, z, g, 0, cut_a, px, 4), copy(5, z, g, cut_a, rows, px, 5)]
    own_y = [copy(8, z, g, cut_a, rows, py, 8), copy(7, z, g, 0, cut_a, py, 7)]

    def to_x(zo):
        return copy(4, zo, g, cut_c, rows, px, 4)

    def to_y(zo):
        return copy(7, zo, g, 0, cut_b, py, 7)

    own_diag = [copy(9, z, gx, 0, cut_a, py, 9), copy(6, z, gy, cut_a, rows, px, 6)]

    def part_c(zo):
        return copy(9, zo, gx, 0, cut_c, py, 9)

    def part_a(zo):
        return copy(11, zo, gx, cut_c, cut_a, py, 11)

    def part_b(zo):
        return copy(10, zo, gy, cut_a, cut_b, px, 10)

    def part_d(zo):
        return copy(6, zo, gy, cut_b, rows, px, 6)

    def got(kind, zo, go, lo, hi):
        copy(kind, zo, go, lo, hi, px, kind).wait_recv()

    spread(0, start)
    own_x[0].start()
    own_y[0].start()
    spread(3, start)
    own_x[1].start()
    own_y[1].start()

    fetch_t.wait()
    steps = features // LANES

    def slabs(c):
        x = tok[:, pl.ds(pl.multiple_of(c * LANES, LANES), LANES)].astype(jnp.float32)
        return [x[:, j:j + 128] for j in range(0, LANES, 128)]

    def add_up(c, total):
        for x in slabs(c):
            total = total + x
        return total

    zero = jnp.zeros((count, 128), jnp.float32)
    mean = jnp.sum(lax.fori_loop(0, steps, add_up, zero), axis=1, keepdims=True) / features

    def squares(c, total):
        for x in slabs(c):
            total = total + (x - mean) * (x - mean)
        return total

    var = jnp.sum(lax.fori_loop(0, steps, squares, zero), axis=1, keepdims=True) / features
    inv = lax.rsqrt(var + 1e-05)

    def normalize(c, carry):
        at = pl.ds(pl.multiple_of(c * LANES, LANES), LANES)
        x = tok[:, at].astype(jnp.float32)
        norm[0:count, at] = ((x - mean) * inv * gain[at][None, :] + bias[at][None, :]).astype(jnp.bfloat16)
        return carry

    lax.fori_loop(0, steps, normalize, 0)

    other = (g, i + 1 - 2 * k)

    def side(p):
        at = pl.ds(pl.multiple_of(p * plane + shift * (1 - k), 128), window)
        return pltpu.make_async_remote_copy(
            src_ref=norm.at[0:count, at], dst_ref=norm.at[count:2 * count, at],
            send_sem=side_send.at[p], recv_sem=side_recv.at[p],
            device_id=other, device_id_type=MESH)

    def side_in(p):
        at = pl.ds(pl.multiple_of(p * plane + shift * k, 128), window)
        return pltpu.make_async_remote_copy(
            src_ref=norm.at[0:count, at], dst_ref=norm.at[count:2 * count, at],
            send_sem=side_send.at[p], recv_sem=side_recv.at[p],
            device_id=other, device_id_type=MESH)

    for p in range(planes):
        side(p).start()

    def product(zo):
        at = pl.multiple_of(zo * plane + shift * k, 128)
        return jnp.dot(norm[:, pl.ds(at, window)], full[pl.ds(at, window), :],
                       preferred_element_type=jnp.float32)

    def whole_in(zo):
        got(0, zo, g, *spans[0])
        forward(0, zo, start)
        got(3, zo, g, *spans[3])
        forward(3, zo, start)
        to_x(zo).start()
        to_y(zo).start()

    def parts_in(zo):
        got(1, zo, gx, *spans[1])
        forward(1, zo, start)
        part_c(zo).start()
        got(2, zo, gy, *spans[2])
        forward(2, zo, start)
        part_d(zo).start()

    def columns_in(zo):
        got(4, zo, gx, cut_c, rows)
        part_a(zo).start()
        got(7, zo, gy, 0, cut_b)
        part_b(zo).start()

    def diagonal_in(zo):
        got(10, zo, gxy, cut_a, cut_b)
        got(11, zo, gxy, cut_c, cut_a)
        got(6, zo, gxy, cut_b, rows)
        got(9, zo, gxy, 0, cut_c)

    low = z < (planes // 2)

    def nth(t):
        mirror = jnp.where(low, z, top - z)
        pick = jnp.where(t - 1 >= mirror, t, t - 1)
        return jnp.where(low, pick, top - pick)

    end = (z == 0) | (z == top)
    got(4, z, gx, 0, cut_a)
    own_diag[0].start()
    got(8, z, gy, cut_a, rows)
    own_diag[1].start()
    whole_in(nth(1))

    @pl.when(end)
    def _():
        spread(1, start)
        spread(2, start)

    for p in range(planes):
        side_in(p).wait_recv()
    for t in range(2, top):
        whole_in(nth(t))
    got(5, z, gx, cut_a, rows)
    got(7, z, gy, 0, cut_a)
    got(6, z, gxy, cut_a, rows)
    got(9, z, gxy, 0, cut_a)
    acc[...] = product(z)
    whole_in(nth(top))

    @pl.when(jnp.logical_not(end))
    def _():
        spread(1, start)
        spread(2, start)

    for t in range(1, planes):
        columns_in(nth(t))
        parts_in(nth(t))
        if t > 1:
            diagonal_in(nth(t - 1))
            acc[...] += product(nth(t - 1))
    diagonal_in(nth(top))
    acc[...] += product(nth(top))

    last = pltpu.make_async_remote_copy(
        src_ref=acc.at[count:2 * count, :], dst_ref=part,
        send_sem=side_send.at[planes], recv_sem=side_recv.at[planes],
        device_id=other, device_id_type=MESH)
    last.start()

    for kind in range(4):
        spread(kind, wait_send)
    for c in own_x + own_y + own_diag:
        c.wait_send()
    for t in range(1, planes):
        zo = nth(t)
        for kind in range(4):
            forward(kind, zo, wait_send)
        for c in (to_x(zo), to_y(zo), part_a(zo), part_b(zo), part_c(zo), part_d(zo)):
            c.wait_send()
    for p in range(planes):
        side(p).wait_send()
    last.wait()
    keys[...] = (acc[0:count, :] + part[...]).astype(keys.dtype)


def gathered_keys(weight, tokens, gain, bias, grps, planes):
    rows, width = weight.shape
    count, features = tokens.shape
    unit = 16
    units = rows // unit
    edge = units // 3
    cuts = (unit * (edge - 1), unit * ((units + 1) // 2), unit * (units - edge))
    anywhere = pl.BlockSpec(memory_space=pl.ANY)
    vmem = pl.BlockSpec(memory_space=pltpu.VMEM)
    return pl.pallas_call(
        functools.partial(gather_kernel, grps, rows, planes, cuts),
        out_shape=jax.ShapeDtypeStruct((count, width), jnp.bfloat16),
        in_specs=[anywhere, anywhere, vmem, vmem],
        out_specs=vmem,
        scratch_shapes=[
            pltpu.VMEM((features, width), jnp.bfloat16),
            pltpu.VMEM((count, features), jnp.bfloat16),
            pltpu.VMEM((2 * count, features), jnp.bfloat16),
            pltpu.VMEM((2 * count, width), jnp.float32),
            pltpu.VMEM((count, width), jnp.float32),
            pltpu.SemaphoreType.DMA((2,)),
            pltpu.SemaphoreType.DMA((12, planes)),
            pltpu.SemaphoreType.DMA((16, planes)),
            pltpu.SemaphoreType.DMA((planes + 1,)),
            pltpu.SemaphoreType.DMA((planes + 1,)),
        ],
        compiler_params=pltpu.CompilerParams(
            collective_id=0, has_side_effects=True, vmem_limit_bytes=60 * 2**20),
        cost_estimate=pl.CostEstimate(
            flops=2 * count * features * width,
            bytes_accessed=2 * count * features + 2 * rows * width,
            transcendentals=0),
    )(weight, tokens, gain, bias)


def kernel_shards(grps, planes, tokens, ln_gain, ln_bias, master, grad, moment1, moment2):
    new_master, new_moment1, new_moment2, weight = adam(master, grad, moment1, moment2)
    keys = gathered_keys(weight, tokens, ln_gain, ln_bias, grps, planes)
    return (new_master, new_moment1, new_moment2, keys)


def solution(mesh):
    grps, members = mesh.shape["grp"], mesh.shape["ing"]

    def body(tokens, ln_gain, ln_bias, master, grad, moment1, moment2):
        rows, width = master.shape
        count, features = tokens.shape
        fits = (
            grps == 4 and members == 8 and rows % 16 == 0 and rows >= 96
            and (8 * rows) % 128 == 0 and width % QBLOCK == 0
            and features % LANES == 0 and count % 16 == 0
        )
        plan = functools.partial(kernel_shards, grps, members // 2) if fits else shards
        return plan(tokens, ln_gain, ln_bias, master, grad, moment1, moment2)

    in_specs = (
        P(("grp", "ing"), None),
        P(),
        P(),
        P(("ing", "grp"), None),
        P(("ing", "grp"), None),
        P(("ing", "grp"), None),
        P(("ing", "grp"), None),
    )
    out_specs = (
        P(("ing", "grp"), None),
        P(("ing", "grp"), None),
        P(("ing", "grp"), None),
        P(("grp", "ing"), None),
    )
    return jax.shard_map(body, mesh=mesh, in_specs=in_specs, out_specs=out_specs, check_vma=False)
```
